256 devices in a mesh: wide: 16 (over z, core), grow: 4 (over y), gcol: 4 (over x).
Axes of the slice: x: 4, y: 4, z: 8, core: 2. Of those that a mesh axis runs over, the one named last changes fastest.
Arguments:
- diag_block: float32 [16, 1024, 1024], P('wide', ('grow', 'gcol')), as said below
- lower_block: float32 [16, 3072, 1024], P('wide', ('grow', 'gcol')), may hold values from -0.1875 to 0.1875
- trailing_block: float32 [16, 3072, 3072], P('wide', 'grow', 'gcol'), as said below
- parent_front: float32 [4, 2048, 8192], P('grow', 'wide', 'gcol'), may hold values from -3 to 3
- row_map: int32 [16, 24], replicated, may hold values from 0 to 63, as said below
Outputs:
- factor: float32 [16, 1024, 1024], P('wide', ('grow', 'gcol'))
- panel: float32 [16, 3072, 1024], P('wide', ('grow', 'gcol'))
- parent: float32 [4, 2048, 8192], P('grow', 'wide', 'gcol')
The draws below stay inside these ranges and needn't reach their ends.
Inputs may be any that keep to these rules, and one draw needn't show every extreme that they name: Each diag_block[g] is symmetric and positive definite. Each trailing_block[g] is symmetric. `row_map`: the blocks of one child are distinct, and child block b goes to a grandparent block p with p // 16 equal to b // 6.
All inputs are finite; a program needn't handle non-finite values.
Results may differ from the reference program's by a relative error of at most 0.0003.
Values sent between devices are 32-bit elements; how exact they have to be, the bound alone decides.
No kernel may reach another device: no remote copies, remote signals or barrier semaphores. Data moves between devices by JAX's collectives and lax.ppermute only.
A program may use at most 128 MiB of HBM per device.

```python
import jax
import jax.numpy as jnp
from jax import lax

NS = 1024
NC = 3072
PN = 8192
BLOCK = 128
GROUPS = 16
QUARTERS = 4
PQ = 2048


def draw_diag_block(key, part):
    noise = jax.random.normal(key, (GROUPS, NS, NS), jnp.float32)
    sym = (noise + jnp.swapaxes(noise, 1, 2)) * (0.5 / NS ** 0.5)
    base = 2.5 + jax.random.uniform(jax.random.fold_in(key, 1), (GROUPS, NS), jnp.float32, 0.0, 1.5)
    matrix = sym + base[:, :, None] * jnp.eye(NS, dtype=jnp.float32)[None]
    return matrix


def draw_trailing_block(key, part):
    noise = jax.random.normal(key, (GROUPS, NC, NC), jnp.float32)
    sym = (noise + jnp.swapaxes(noise, 1, 2)) * (0.5 / NC ** 0.5)
    base = jax.random.uniform(jax.random.fold_in(key, 1), (GROUPS, NC), jnp.float32, 0.5, 1.5)
    return sym + base[:, :, None] * jnp.eye(NC, dtype=jnp.float32)[None]


def draw_row_map(key, part):
    quarter_blocks = PN // (BLOCK * QUARTERS)
    child_blocks = NC // (BLOCK * QUARTERS)
    keys = jax.random.split(jax.random.fold_in(key, 7), GROUPS * QUARTERS)
    orders = jax.vmap(lambda single: jax.random.permutation(single, quarter_blocks))(keys)
    picked = orders[:, :child_blocks].reshape(GROUPS, QUARTERS, child_blocks)
    shifted = picked + (jnp.arange(QUARTERS, dtype=jnp.int32) * quarter_blocks)[None, :, None]
    return shifted.reshape(GROUPS, QUARTERS * child_blocks).astype(jnp.int32)


def levels(rng, dims, cuts, least, largest):
    level = 1.0
    for dim, parts in cuts:
        steps = jax.random.uniform(jax.random.fold_in(jax.random.fold_in(rng, 6), dim), (parts,), jnp.float32, least / len(cuts), largest / len(cuts))
        level = level * jnp.repeat(jnp.exp(steps), dims[dim] // parts).reshape((-1,) + (1,) * (len(dims) - 1 - dim))
    return level


def gaussian(own_key, shape, width, reach, shards=(), kind=jnp.bfloat16):
    factor_of = levels(own_key, shape, shards, -0.22, 0.18) if shards else 1.0
    values = jax.random.normal(own_key, shape, jnp.float32) * width * factor_of
    return jnp.minimum(jnp.maximum(values, -reach), reach).astype(kind)


def setup_inputs(seed: int = 0) -> dict:
    arg_keys = jax.random.split(jax.random.key(seed), 6)
    diag_block = draw_diag_block(jax.random.fold_in(arg_keys[5], 71), 0)
    lower_block = gaussian(arg_keys[1], (GROUPS, NC, NS), NS ** -0.5, 0.1875, ((0, 16), (1, 16)), jnp.float32)
    trailing_block = draw_trailing_block(jax.random.fold_in(arg_keys[5], 71), 0)
    parent_front = gaussian(arg_keys[3], (QUARTERS, PQ, PN), 0.5, 3.0, ((0, 4), (1, 16), (2, 4)), jnp.float32)
    row_map = draw_row_map(jax.random.fold_in(arg_keys[5], 71), 0)
    return {"diag_block": diag_block, "lower_block": lower_block, "trailing_block": trailing_block, "parent_front": parent_front, "row_map": row_map}


def reference(diag_block, lower_block, trailing_block, parent_front, row_map):
    factor = jnp.linalg.cholesky(diag_block)
    solved = jax.scipy.linalg.solve_triangular(factor, jnp.swapaxes(lower_block, 1, 2), lower=True)
    panel = jnp.swapaxes(solved, 1, 2)
    schur = trailing_block - jnp.einsum('gik,gjk->gij', panel, panel, precision=lax.Precision.HIGHEST)
    order = parent_front.shape[0] * parent_front.shape[1]
    offsets = jnp.arange(BLOCK, dtype=jnp.int32)

    def add_child(total, item):
        contribution, blocks = item
        index = (blocks.astype(jnp.int32)[:, None] * BLOCK + offsets[None, :]).reshape(-1)
        return (total.at[index[:, None], index[None, :]].add(contribution), None)
    total, _ = lax.scan(add_child, parent_front.reshape(order, order), (schur, row_map))
    return (factor, panel, total.reshape(parent_front.shape))
```

```python
import functools

import jax
import jax.numpy as jnp
from jax import lax
from jax.experimental import pallas as pl
from jax.experimental.pallas import tpu as pltpu
from jax.sharding import PartitionSpec as P

BLOCK = 128
WIDE = 256
SUB = 8
VMEM = pl.BlockSpec(memory_space=pltpu.VMEM)
PARAMS = pltpu.CompilerParams(vmem_limit_bytes=56 * 2**20)


def dot_nt(x, y):
    return lax.dot_general(
        x,
        y,
        (((1,), (1,)), ((), ())),
        precision=lax.Precision.HIGHEST,
        preferred_element_type=jnp.float32,
    )


def split(x):
    high = x.astype(jnp.bfloat16)
    return high, (x - high.astype(jnp.float32)).astype(jnp.bfloat16)


def dot_split(x, y):
    def one(a, b):
        return lax.dot_general(
            a, b, (((1,), (1,)), ((), ())), preferred_element_type=jnp.float32
        )

    return one(x[0], y[0]) + (one(x[0], y[1]) + one(x[1], y[0]))


def factor_block(rows):
    count = len(rows)
    shape = (SUB, BLOCK)
    lane = lax.broadcasted_iota(jnp.int32, shape, 1)
    sub = lax.broadcasted_iota(jnp.int32, shape, 0)
    left = list(rows)
    right = [jnp.where(lane == sub + SUB * b, 1.0, 0.0).astype(jnp.float32) for b in range(count)]

    def along_lanes(x, j):
        return jnp.broadcast_to(x[:, j : j + 1], shape)

    def along_rows(x, j):
        return jnp.broadcast_to(x[j : j + 1, :], shape)

    for b in range(count):
        columns = [along_lanes(left[b], SUB * b + j) for j in range(SUB)]
        t = [[along_rows(columns[j], i) for j in range(i + 1)] for i in range(SUB)]
        inverse = []
        for j in range(SUB):
            inverse.append(lax.rsqrt(t[j][j]))
            for i in range(j + 1, SUB):
                t[i][j] = t[i][j] * inverse[j]
            for i in range(j + 1, SUB):
                for k in range(j + 1, i + 1):
                    t[i][k] = t[i][k] - t[i][j] * t[k][j]

        def solve(values):
            out = []
            for j in range(SUB):
                value = values[j]
                for k in range(j):
                    value = value - t[j][k] * out[k]
                out.append(value * inverse[j])
            return out

        upper = solve([along_rows(left[b], j) for j in range(SUB)])
        lower = solve([along_rows(right[b], j) for j in range(SUB)])
        left_b, right_b = upper[0], lower[0]
        for j in range(1, SUB):
            left_b = jnp.where(sub == j, upper[j], left_b)
            right_b = jnp.where(sub == j, lower[j], right_b)
        left[b], right[b] = left_b, right_b
        for c in range(b + 1, count):
            scale = solve([along_lanes(left[c], SUB * b + j) for j in range(SUB)])
            for j in range(SUB):
                left[c] = left[c] - scale[j] * upper[j]
                right[c] = right[c] - scale[j] * lower[j]
    return left, right


def factor_kernel(a_ref, l_ref, w_ref, s_ref):
    n = a_ref.shape[0]
    ii = lax.broadcasted_iota(jnp.int32, (BLOCK, BLOCK), 0)
    jj = lax.broadcasted_iota(jnp.int32, (BLOCK, BLOCK), 1)
    for o in range(0, n, BLOCK):
        src = s_ref if o else a_ref
        e = o + BLOCK
        upper, inverse = factor_block([src[o + r : o + r + SUB, o:e] for r in range(0, BLOCK, SUB)])
        l_ref[o:e, o:e] = jnp.where(ii >= jj, jnp.concatenate(upper, axis=0).T, 0.0)
        inverse = jnp.concatenate(inverse, axis=0)
        w_ref[o // BLOCK] = inverse
        if o:
            l_ref[0:o, o:e] = jnp.zeros((o, BLOCK), jnp.float32)
        if e == n:
            break
        below = dot_nt(src[e:, o:e], inverse)
        l_ref[e:, o:e] = below
        for j in range(e, n, BLOCK):
            update = dot_nt(below[j - e :], below[j - e : j - e + BLOCK])
            s_ref[j:, j : j + BLOCK] = src[j:, j : j + BLOCK] - update


def factor_whole(a):
    n = a.shape[0]
    return pl.pallas_call(
        factor_kernel,
        name="factor",
        out_shape=(
            jax.ShapeDtypeStruct((n, n), jnp.float32),
            jax.ShapeDtypeStruct((n // BLOCK, BLOCK, BLOCK), jnp.float32),
        ),
        in_specs=[VMEM],
        out_specs=(VMEM, VMEM),
        scratch_shapes=[pltpu.VMEM((n, n), jnp.float32)],
        compiler_params=PARAMS,
        cost_estimate=pl.CostEstimate(
            flops=40 * n**3, bytes_accessed=400 * n * n, transcendentals=0
        ),
    )(a)


def solve_kernel(l_ref, w_ref, row_ref, col_ref, t_ref, p_ref, s_ref, high, low):
    n = l_ref.shape[0]
    m = row_ref.shape[0]
    for j in range(0, n, WIDE):
        half = j + BLOCK
        e = j + WIDE
        w0, w1 = w_ref[j // BLOCK], w_ref[half // BLOCK]
        cross = lax.dot_general(
            w1,
            lax.dot_general(
                l_ref[half:e, j:half],
                w0,
                (((1,), (0,)), ((), ())),
                precision=lax.Precision.HIGHEST,
                preferred_element_type=jnp.float32,
            ),
            (((1,), (0,)), ((), ())),
            precision=lax.Precision.HIGHEST,
            preferred_element_type=jnp.float32,
        )
        zero = jnp.zeros((BLOCK, BLOCK), jnp.float32)
        w = split(
            jnp.concatenate(
                [
                    jnp.concatenate([w0, zero], axis=1),
                    jnp.concatenate([-cross, w1], axis=1),
                ],
                axis=0,
            )
        )
        if j:
            left = split(l_ref[j:e, 0:j])
        for start, ref in ((0, row_ref), (m, col_ref)):
            value = ref[:, j:e]
            rows = slice(start, start + m)
            if j:
                value = value - dot_split((high[rows, 0:j], low[rows, 0:j]), left)
            value = dot_split(split(value), w)
            if start == 0:
                p_ref[:, j:e] = value
            value = split(value)
            high[rows, j:e] = value[0]
            low[rows, j:e] = value[1]
    s_ref[...] = t_ref[...] - dot_split((high[0:m], low[0:m]), (high[m:], low[m:]))


def solve_and_update(factor, inverses, rows, columns, trailing):
    m, n = rows.shape
    return pl.pallas_call(
        solve_kernel,
        name="solve",
        out_shape=(
            jax.ShapeDtypeStruct((m, n), jnp.float32),
            jax.ShapeDtypeStruct((m, m), jnp.float32),
        ),
        in_specs=[VMEM] * 5,
        out_specs=(VMEM, VMEM),
        scratch_shapes=[pltpu.VMEM((2 * m, n), jnp.bfloat16)] * 2,
        compiler_params=PARAMS,
        cost_estimate=pl.CostEstimate(
            flops=6 * m * n * (n + m), bytes_accessed=4 * (3 * m * n + n * n), transcendentals=0
        ),
    )(factor, inverses, rows, columns, trailing)


def place_kernel(where_ref, s_ref, o_ref, *, blocks):
    o_ref[...] = jnp.zeros_like(o_ref)

    @pl.when(where_ref[pl.program_id(0)] >= 0)
    def _():
        for b in range(s_ref.shape[1] // BLOCK):
            column = where_ref[blocks + b]
            o_ref[:, pl.ds(pl.multiple_of(column * BLOCK, BLOCK), BLOCK)] = s_ref[
                :, b * BLOCK : (b + 1) * BLOCK
            ]


def place(schur, where, blocks, width):
    return pl.pallas_call(
        functools.partial(place_kernel, blocks=blocks),
        name="place",
        out_shape=jax.ShapeDtypeStruct((blocks * BLOCK, width), jnp.float32),
        grid_spec=pltpu.PrefetchScalarGridSpec(
            num_scalar_prefetch=1,
            grid=(blocks,),
            in_specs=[
                pl.BlockSpec(
                    (BLOCK, schur.shape[1]), lambda r, where: (jnp.maximum(where[r], 0), 0)
                )
            ],
            out_specs=pl.BlockSpec((BLOCK, width), lambda r, where: (r, 0)),
        ),
        compiler_params=PARAMS,
    )(where, schur)


def local(diag_block, lower_block, trailing_block, parent_front, row_map):
    grow, gcol = lax.axis_index("grow"), lax.axis_index("gcol")
    side = lax.axis_size("gcol")
    whole = lax.all_gather(diag_block[0], ("grow", "gcol"), axis=0, tiled=True)
    whole, lower = lax.optimization_barrier((whole, lower_block[0]))
    rows = lax.all_gather(lower, "gcol", axis=0, tiled=True)
    swap = [(i * side + j, j * side + i) for i in range(side) for j in range(side)]
    turned = lax.ppermute(lower, ("grow", "gcol"), swap)
    columns = lax.all_gather(turned, "grow", axis=0, tiled=True)

    factor, inverses = factor_whole(whole)
    share = diag_block.shape[1]
    factor_rows = lax.dynamic_slice_in_dim(factor, (grow * side + gcol) * share, share, 0)
    solved, schur = solve_and_update(factor, inverses, rows, columns, trailing_block[0])
    own = lower_block.shape[1]
    panel = lax.dynamic_slice_in_dim(solved, gcol * own, own, 0)

    width_blocks = schur.shape[0] // BLOCK
    blocks = parent_front.shape[1] * lax.axis_size("wide") // BLOCK
    mine = lax.dynamic_slice_in_dim(row_map, lax.axis_index("wide"), 1, 0)[0]
    row_to = lax.dynamic_slice_in_dim(mine, grow * width_blocks, width_blocks) % blocks
    col_to = lax.dynamic_slice_in_dim(mine, gcol * width_blocks, width_blocks) % blocks
    hit = row_to[None, :] == jnp.arange(blocks, dtype=jnp.int32)[:, None]
    row_from = jnp.max(jnp.where(hit, jnp.arange(width_blocks, dtype=jnp.int32)[None], -1), axis=1)
    where = jnp.concatenate([row_from, col_to])
    spread = place(schur, where, blocks, parent_front.shape[2])
    summed = lax.psum_scatter(spread, "wide", scatter_dimension=0, tiled=True)
    parent = parent_front + summed[None]
    return factor_rows[None], panel[None], parent


def solution(mesh):
    placed = (
        P("wide", ("grow", "gcol"), None),
        P("wide", ("grow", "gcol"), None),
        P("wide", "grow", "gcol"),
        P("grow", "wide", "gcol"),
        P(),
    )
    return jax.shard_map(
        local,
        mesh=mesh,
        in_specs=placed,
        out_specs=(
            P("wide", ("grow", "gcol"), None),
            P("wide", ("grow", "gcol"), None),
            P("grow", "wide", "gcol"),
        ),
        check_vma=False,
    )
```

```python
import functools

import jax
import jax.numpy as jnp
from jax import lax
from jax.experimental import pallas as pl
from jax.experimental.pallas import tpu as pltpu
from jax.sharding import PartitionSpec as P

BLOCK = 128
WIDE = 256
SUB = 8
VMEM = pl.BlockSpec(memory_space=pltpu.VMEM)
ANY = pl.BlockSpec(memory_space=pl.ANY)
SMEM = pl.BlockSpec(memory_space=pltpu.SMEM)
PARAMS = pltpu.CompilerParams(vmem_limit_bytes=56 * 2**20)


def dot_nt(x, y):
    return lax.dot_general(
        x,
        y,
        (((1,), (1,)), ((), ())),
        precision=lax.Precision.HIGHEST,
        preferred_element_type=jnp.float32,
    )


def split(x):
    high = x.astype(jnp.bfloat16)
    return high, (x - high.astype(jnp.float32)).astype(jnp.bfloat16)


def dot_split(x, y):
    def one(a, b):
        return lax.dot_general(
            a, b, (((1,), (1,)), ((), ())), preferred_element_type=jnp.float32
        )

    return one(x[0], y[0]) + (one(x[0], y[1]) + one(x[1], y[0]))


def factor_block(rows):
    count = len(rows)
    shape = (SUB, BLOCK)
    lane = lax.broadcasted_iota(jnp.int32, shape, 1)
    sub = lax.broadcasted_iota(jnp.int32, shape, 0)
    left = list(rows)
    right = [jnp.where(lane == sub + SUB * b, 1.0, 0.0).astype(jnp.float32) for b in range(count)]

    def along_lanes(x, j):
        return jnp.broadcast_to(x[:, j : j + 1], shape)

    def along_rows(x, j):
        return jnp.broadcast_to(x[j : j + 1, :], shape)

    for b in range(count):
        columns = [along_lanes(left[b], SUB * b + j) for j in range(SUB)]
        t = [[along_rows(columns[j], i) for j in range(i + 1)] for i in range(SUB)]
        inverse = []
        for j in range(SUB):
            inverse.append(lax.rsqrt(t[j][j]))
            for i in range(j + 1, SUB):
                t[i][j] = t[i][j] * inverse[j]
            for i in range(j + 1, SUB):
                for k in range(j + 1, i + 1):
                    t[i][k] = t[i][k] - t[i][j] * t[k][j]

        def solve(values):
            out = []
            for j in range(SUB):
                value = values[j]
                for k in range(j):
                    value = value - t[j][k] * out[k]
                out.append(value * inverse[j])
            return out

        upper = solve([along_rows(left[b], j) for j in range(SUB)])
        lower = solve([along_rows(right[b], j) for j in range(SUB)])
        left_b, right_b = upper[0], lower[0]
        for j in range(1, SUB):
            left_b = jnp.where(sub == j, upper[j], left_b)
            right_b = jnp.where(sub == j, lower[j], right_b)
        left[b], right[b] = left_b, right_b
        for c in range(b + 1, count):
            scale = solve([along_lanes(left[c], SUB * b + j) for j in range(SUB)])
            for j in range(SUB):
                left[c] = left[c] - scale[j] * upper[j]
                right[c] = right[c] - scale[j] * lower[j]
    return left, right


def sweep(start, stop, end, place, l_ref, w_ref):
    ii = lax.broadcasted_iota(jnp.int32, (BLOCK, BLOCK), 0)
    jj = lax.broadcasted_iota(jnp.int32, (BLOCK, BLOCK), 1)
    for o in range(start, stop, BLOCK):
        e = o + BLOCK
        ref, r, c = place(o)
        upper, inverse = factor_block(
            [ref[r + k : r + k + SUB, c : c + BLOCK] for k in range(0, BLOCK, SUB)]
        )
        at = slice(o - start, e - start)
        l_ref[at, at] = jnp.where(ii >= jj, jnp.concatenate(upper, axis=0).T, 0.0)
        inverse = jnp.concatenate(inverse, axis=0)
        w_ref[(o - start) // BLOCK] = inverse
        if o > start:
            l_ref[0 : o - start, at] = jnp.zeros((o - start, BLOCK), jnp.float32)
        if e == end:
            break
        below = dot_nt(ref[r + BLOCK : r + end - o, c : c + BLOCK], inverse)
        l_ref[e - start :, at] = below
        for j in range(e, end, BLOCK):
            update = dot_nt(below[j - e :], below[j - e : j - e + BLOCK])
            ref, r, c = place(j)
            here = (slice(r, r + end - j), slice(c, c + BLOCK))
            ref[here] = ref[here] - update


def first_kernel(info_ref, *refs, side, shifts):
    pieces, (l_ref, w_ref, rest_ref, g_ref, s_ref, sems) = refs[: 2 * side], refs[2 * side :]
    n = g_ref.shape[0]
    steps = n // BLOCK
    slots = g_ref.shape[1] // BLOCK
    share = n // side**2
    part = share // 2
    half = l_ref.shape[1]
    grow, gcol = info_ref[0], info_ref[1]
    copies = []
    for way in range(2):
        for u in range(side):
            for t in range(side):
                di, dj = (shifts[u], shifts[t]) if way == 0 else (shifts[t], shifts[u])
                spot = lax.rem(grow + side - di, side) * side + lax.rem(gcol + side - dj, side)
                to = pl.multiple_of(spot * share + way * part, part)
                copies.append(
                    pltpu.make_async_copy(
                        pieces[way * side + u].at[t * part : (t + 1) * part],
                        g_ref.at[pl.ds(to, part)],
                        sems.at[len(copies)],
                    )
                )
    for copy in copies:
        copy.start()
    for copy in copies:
        copy.wait()

    def place(j):
        return (s_ref, j, j) if j < half else (rest_ref, j - half, j - half)

    for k in range(steps):
        ref, r, c = place(k * BLOCK)
        own = slice(k * BLOCK, (k + 1) * BLOCK)
        for i in range(k, steps):
            if i - k < slots:
                value = g_ref[i * BLOCK : (i + 1) * BLOCK, (i - k) * BLOCK : (i - k + 1) * BLOCK]
            else:
                m = (k - i + steps) * BLOCK
                value = g_ref[own, m : m + BLOCK].T
            ref[r + (i - k) * BLOCK : r + (i - k + 1) * BLOCK, c : c + BLOCK] = value
    sweep(0, half, n, place, l_ref, w_ref)


def second_kernel(rest_ref, l_ref, w_ref, s_ref):
    n = rest_ref.shape[0]
    for k in range(0, n, BLOCK):
        s_ref[k:, k : k + BLOCK] = rest_ref[k:, k : k + BLOCK]
    sweep(0, n, n, lambda j: (s_ref, j, j), l_ref, w_ref)


def shape(*dims):
    return jax.ShapeDtypeStruct(dims, jnp.float32)


def factor_first(info, pieces, n, side, shifts):
    half = n // 2
    slots = n // BLOCK // 2 + 1
    return pl.pallas_call(
        functools.partial(first_kernel, side=side, shifts=shifts),
        name="factor_first",
        out_shape=(shape(n, half), shape(half // BLOCK, BLOCK, BLOCK), shape(half, half)),
        in_specs=[SMEM] + [ANY] * len(pieces),
        out_specs=(VMEM, VMEM, VMEM),
        scratch_shapes=[
            pltpu.VMEM((n, slots * BLOCK), jnp.float32),
            pltpu.VMEM((n, half), jnp.float32),
            pltpu.SemaphoreType.DMA((2 * side**2,)),
        ],
        compiler_params=PARAMS,
        cost_estimate=pl.CostEstimate(
            flops=20 * n**3, bytes_accessed=100 * n * n, transcendentals=0
        ),
    )(info, *pieces)


def factor_second(rest):
    n = rest.shape[0]
    return pl.pallas_call(
        second_kernel,
        name="factor_second",
        out_shape=(shape(n, n), shape(n // BLOCK, BLOCK, BLOCK)),
        in_specs=[VMEM],
        out_specs=(VMEM, VMEM),
        scratch_shapes=[pltpu.VMEM((n, n), jnp.float32)],
        compiler_params=PARAMS,
        cost_estimate=pl.CostEstimate(
            flops=160 * n**3, bytes_accessed=400 * n * n, transcendentals=0
        ),
    )(rest)


def dot_nn(x, y):
    return lax.dot_general(
        x,
        y,
        (((1,), (0,)), ((), ())),
        precision=lax.Precision.HIGHEST,
        preferred_element_type=jnp.float32,
    )


def solve_kernel(info_ref, l0_ref, l1_ref, w0_ref, w1_ref, *refs, side, shifts, blocks):
    row_hbm, col_hbm, t_hbm = refs[0], refs[1 : 1 + side], refs[1 + side]
    p_ref, o_ref, rows, cols, s_ref, high, low, z_ref, sems, zero_sem = refs[2 + side :]
    half, n = l1_ref.shape[0], l0_ref.shape[0]
    m = rows.shape[0]
    own = m // side
    count = m // BLOCK
    grow, gcol = info_ref[0], info_ref[1]
    row_from, col_from = 2, 2 + blocks
    row_to = 2 + 2 * blocks
    col_to = row_to + count

    loads = [pltpu.make_async_copy(row_hbm, rows, sems.at[0])]
    for k in range(side):
        to = pl.multiple_of(lax.rem(grow + side - shifts[k], side) * own, own)
        loads.append(
            pltpu.make_async_copy(col_hbm[k], cols.at[pl.ds(to, own)], sems.at[1 + k])
        )
    loads.append(pltpu.make_async_copy(t_hbm, s_ref, sems.at[1 + side]))
    for load in loads:
        load.start()
    z_ref[...] = jnp.zeros_like(z_ref)

    def zeros(act):
        def row(r, _):
            here = pl.ds(pl.multiple_of(r * BLOCK, BLOCK), BLOCK)
            absent = info_ref[row_from + r] < 0

            @pl.when(absent)
            def _():
                act(pltpu.make_async_copy(z_ref, o_ref.at[here], zero_sem))

            @pl.when(jnp.logical_not(absent))
            def _():
                def block(c, _):
                    @pl.when(info_ref[col_from + c] < 0)
                    def _():
                        there = pl.ds(pl.multiple_of(c * BLOCK, BLOCK), BLOCK)
                        act(
                            pltpu.make_async_copy(
                                z_ref.at[:, 0:BLOCK], o_ref.at[here, there], zero_sem
                            )
                        )

                    return 0

                lax.fori_loop(0, blocks, block, 0)

            return 0

        lax.fori_loop(0, blocks, row, 0)

    zeros(lambda copy: copy.start())

    def inverse(k):
        return w0_ref[k] if k < half // BLOCK else w1_ref[k - half // BLOCK]

    def factor(r, c):
        return l0_ref[r, c] if c.start < half else l1_ref[
            slice(r.start - half, r.stop - half), slice(c.start - half, c.stop - half)
        ]

    kept = []
    for part, value_ref in ((0, rows), (1, cols)):
        base = part * m
        at = slice(base, base + m)
        if part == 0:
            loads[0].wait()
        else:
            for load in loads[1 : 1 + side]:
                load.wait()
        for j in range(0, n, WIDE):
            mid, e = j + BLOCK, j + WIDE
            if part == 0:
                w0, w1 = inverse(j // BLOCK), inverse(mid // BLOCK)
                cross = dot_nn(w1, dot_nn(factor(slice(mid, e), slice(j, mid)), w0))
                zero = jnp.zeros((BLOCK, BLOCK), jnp.float32)
                top = jnp.concatenate([w0, zero], axis=1)
                both = split(
                    jnp.concatenate([top, jnp.concatenate([-cross, w1], axis=1)], axis=0)
                )
                kept.append(both)
            w = kept[j // WIDE]
            value = value_ref[:, j:e]
            if j:
                c = min(j, half)
                left = split(l0_ref[j:e, 0:c])
                value = value - dot_split((high[at, 0:c], low[at, 0:c]), left)
            if j > half:
                left = split(l1_ref[j - half : e - half, 0 : j - half])
                value = value - dot_split((high[at, half:j], low[at, half:j]), left)
            value = dot_split(split(value), w)
            if part == 0:
                rows[:, j:e] = value
            value = split(value)
            high[at, j:e] = value[0]
            low[at, j:e] = value[1]
        if part == 0:
            p_ref[...] = rows[pl.ds(pl.multiple_of(gcol * own, own), own), :]

    loads[1 + side].wait()
    stores = []
    step = m // 2
    for r in range(0, m, step):
        here = slice(r, r + step)
        s_ref[here, :] = s_ref[here, :] - dot_split(
            (high[here, :], low[here, :]), (high[m:, :], low[m:, :])
        )
        for a in range(r // BLOCK, (r + step) // BLOCK):
            there = pl.ds(pl.multiple_of(info_ref[row_to + a] * BLOCK, BLOCK), BLOCK)
            for b in range(count):
                column = pl.ds(pl.multiple_of(info_ref[col_to + b] * BLOCK, BLOCK), BLOCK)
                copy = pltpu.make_async_copy(
                    s_ref.at[a * BLOCK : (a + 1) * BLOCK, b * BLOCK : (b + 1) * BLOCK],
                    o_ref.at[there, column],
                    sems.at[2 + side + len(stores)],
                )
                copy.start()
                stores.append(copy)
    for copy in stores:
        copy.wait()
    zeros(lambda copy: copy.wait())


def solve_and_place(info, factors, inverses, rows, columns, trailing, blocks, shifts):
    m, n = rows.shape
    side = len(columns)
    count = m // BLOCK
    return pl.pallas_call(
        functools.partial(solve_kernel, side=side, shifts=shifts, blocks=blocks),
        name="solve",
        out_shape=(shape(m // side, n), shape(blocks * BLOCK, blocks * BLOCK)),
        in_specs=[SMEM] + [VMEM] * 4 + [ANY] * (2 + side),
        out_specs=(VMEM, ANY),
        scratch_shapes=[
            pltpu.VMEM((m, n), jnp.float32),
            pltpu.VMEM((m, n), jnp.float32),
            pltpu.VMEM((m, m), jnp.float32),
            pltpu.VMEM((2 * m, n), jnp.bfloat16),
            pltpu.VMEM((2 * m, n), jnp.bfloat16),
            pltpu.VMEM((BLOCK, blocks * BLOCK), jnp.float32),
            pltpu.SemaphoreType.DMA((2 + side + count**2,)),
            pltpu.SemaphoreType.DMA,
        ],
        compiler_params=PARAMS,
        cost_estimate=pl.CostEstimate(
            flops=6 * m * n * (n + m), bytes_accessed=4 * (3 * m * n + n * n), transcendentals=0
        ),
    )(info, *factors, *inverses, rows, *columns, trailing)


def packed_rows(rows, index, parts):
    n = rows.shape[1]
    steps = n // BLOCK
    slots = steps // 2 + 1
    own = index * steps // parts
    twice = jnp.concatenate([rows, rows], axis=1)
    start = (own + steps - slots + 1) % steps
    turned = lax.dynamic_slice_in_dim(twice, start * BLOCK, slots * BLOCK, 1)
    pieces = [turned[:, (slots - 1 - m) * BLOCK : (slots - m) * BLOCK] for m in range(slots)]
    return jnp.concatenate(pieces, axis=1)


def around(x, axis, shifts):
    size = lax.axis_size(axis)
    return [
        lax.ppermute(x, axis, [(s, (s + t) % size) for s in range(size)]) if t else x
        for t in shifts
    ]


def local(diag_block, lower_block, trailing_block, parent_front, row_map):
    grow, gcol = lax.axis_index("grow"), lax.axis_index("gcol")
    side = lax.axis_size("gcol")
    spot = grow * side + gcol
    shifts = (0, 1, side - 1) + tuple(range(2, side - 1))
    lower = lower_block[0]
    trailing = trailing_block[0]
    n = diag_block.shape[2]
    half = n // 2

    count = trailing.shape[0] // BLOCK
    blocks = parent_front.shape[1] * lax.axis_size("wide") // BLOCK
    mine = lax.dynamic_slice_in_dim(row_map, lax.axis_index("wide"), 1, 0)[0]
    targets = [
        lax.dynamic_slice_in_dim(mine, k * count, count) % blocks for k in (grow, gcol)
    ]
    slots = jnp.arange(blocks, dtype=jnp.int32)[:, None]
    sources = [
        jnp.max(
            jnp.where(to[None, :] == slots, jnp.arange(count, dtype=jnp.int32)[None], -1), axis=1
        )
        for to in targets
    ]
    info = jnp.concatenate([jnp.stack([grow, gcol]).astype(jnp.int32), *sources, *targets])

    swap = [(i * side + j, j * side + i) for i in range(side) for j in range(side)]
    packed = packed_rows(diag_block[0], spot, side * side)
    part = packed.shape[0] // 2
    top = jnp.concatenate(around(packed[:part], "gcol", shifts), axis=0)
    bottom = jnp.concatenate(around(packed[part:], "grow", shifts), axis=0)
    pieces = around(top, "grow", shifts) + around(bottom, "gcol", shifts)
    pieces, lower = lax.optimization_barrier((pieces, lower))
    turned = lax.ppermute(lower, ("grow", "gcol"), swap)
    rows = lax.all_gather(lower, "gcol", axis=0, tiled=True)
    l0, w0, rest = factor_first(info, pieces, n, side, shifts)
    rest, turned = lax.optimization_barrier((rest, turned))
    columns = around(turned, "grow", shifts)
    l1, w1 = factor_second(rest)
    share = diag_block.shape[1]
    own_rows = lax.dynamic_slice_in_dim(l0, spot * share, share, 0)
    late = jnp.maximum(spot * share - half, 0)
    right = lax.dynamic_slice_in_dim(l1, late, share, 0)
    right = jnp.where(spot * share >= half, right, 0.0)
    factor_rows = jnp.concatenate([own_rows, right], axis=1)

    panel, spread = solve_and_place(
        info, (l0, l1), (w0, w1), rows, columns, trailing, blocks, shifts
    )
    summed = lax.psum_scatter(spread, "wide", scatter_dimension=0, tiled=True)
    parent = parent_front + summed[None]
    return factor_rows[None], panel[None], parent


def solution(mesh):
    placed = (
        P("wide", ("grow", "gcol"), None),
        P("wide", ("grow", "gcol"), None),
        P("wide", "grow", "gcol"),
        P("grow", "wide", "gcol"),
        P(),
    )
    return jax.shard_map(
        local,
        mesh=mesh,
        in_specs=placed,
        out_specs=(
            P("wide", ("grow", "gcol"), None),
            P("wide", ("grow", "gcol"), None),
            P("grow", "wide", "gcol"),
        ),
        check_vma=False,
    )
```

```python
import functools

import jax
import jax.numpy as jnp
from jax import lax
from jax.experimental import pallas as pl
from jax.experimental.pallas import tpu as pltpu
from jax.sharding import PartitionSpec as P

BLOCK = 128
WIDE = 256
SUB = 8
VMEM = pl.BlockSpec(memory_space=pltpu.VMEM)
ANY = pl.BlockSpec(memory_space=pl.ANY)
SMEM = pl.BlockSpec(memory_space=pltpu.SMEM)
PARAMS = pltpu.CompilerParams(vmem_limit_bytes=56 * 2**20)


def dot_nt(x, y):
    return lax.dot_general(
        x,
        y,
        (((1,), (1,)), ((), ())),
        precision=lax.Precision.HIGHEST,
        preferred_element_type=jnp.float32,
    )


def split(x):
    high = x.astype(jnp.bfloat16)
    return high, (x - high.astype(jnp.float32)).astype(jnp.bfloat16)


def dot_split(x, y):
    def one(a, b):
        return lax.dot_general(
            a, b, (((1,), (1,)), ((), ())), preferred_element_type=jnp.float32
        )

    return one(x[0], y[0]) + (one(x[0], y[1]) + one(x[1], y[0]))


def factor_block(rows):
    count = len(rows)
    shape = (SUB, BLOCK)
    lane = lax.broadcasted_iota(jnp.int32, shape, 1)
    sub = lax.broadcasted_iota(jnp.int32, shape, 0)
    left = list(rows)
    right = [jnp.where(lane == sub + SUB * b, 1.0, 0.0).astype(jnp.float32) for b in range(count)]

    def along_lanes(x, j):
        return jnp.broadcast_to(x[:, j : j + 1], shape)

    def along_rows(x, j):
        return jnp.broadcast_to(x[j : j + 1, :], shape)

    for b in range(count):
        columns = [along_lanes(left[b], SUB * b + j) for j in range(SUB)]
        t = [[along_rows(columns[j], i) for j in range(i + 1)] for i in range(SUB)]
        inverse = []
        for j in range(SUB):
            inverse.append(lax.rsqrt(t[j][j]))
            for i in range(j + 1, SUB):
                t[i][j] = t[i][j] * inverse[j]
            for i in range(j + 1, SUB):
                for k in range(j + 1, i + 1):
                    t[i][k] = t[i][k] - t[i][j] * t[k][j]

        def solve(values):
            out = []
            for j in range(SUB):
                value = values[j]
                for k in range(j):
                    value = value - t[j][k] * out[k]
                out.append(value * inverse[j])
            return out

        upper = solve([along_rows(left[b], j) for j in range(SUB)])
        lower = solve([along_rows(right[b], j) for j in range(SUB)])
        left_b, right_b = upper[0], lower[0]
        for j in range(1, SUB):
            left_b = jnp.where(sub == j, upper[j], left_b)
            right_b = jnp.where(sub == j, lower[j], right_b)
        left[b], right[b] = left_b, right_b
        for c in range(b + 1, count):
            scale = solve([along_lanes(left[c], SUB * b + j) for j in range(SUB)])
            for j in range(SUB):
                left[c] = left[c] - scale[j] * upper[j]
                right[c] = right[c] - scale[j] * lower[j]
    return left, right


def sweep(start, stop, end, place, l_ref, w_ref):
    ii = lax.broadcasted_iota(jnp.int32, (BLOCK, BLOCK), 0)
    jj = lax.broadcasted_iota(jnp.int32, (BLOCK, BLOCK), 1)
    for o in range(start, stop, BLOCK):
        e = o + BLOCK
        ref, r, c = place(o)
        upper, inverse = factor_block(
            [ref[r + k : r + k + SUB, c : c + BLOCK] for k in range(0, BLOCK, SUB)]
        )
        at = slice(o - start, e - start)
        l_ref[at, at] = jnp.where(ii >= jj, jnp.concatenate(upper, axis=0).T, 0.0)
        inverse = jnp.concatenate(inverse, axis=0)
        w_ref[(o - start) // BLOCK] = inverse
        if o > start:
            l_ref[0 : o - start, at] = jnp.zeros((o - start, BLOCK), jnp.float32)
        if e == end:
            break
        below = dot_nt(ref[r + BLOCK : r + end - o, c : c + BLOCK], inverse)
        l_ref[e - start :, at] = below
        for j in range(e, end, BLOCK):
            update = dot_nt(below[j - e :], below[j - e : j - e + BLOCK])
            ref, r, c = place(j)
            here = (slice(r, r + end - j), slice(c, c + BLOCK))
            ref[here] = ref[here] - update


def first_kernel(info_ref, *refs, side, shifts):
    pieces, (l_ref, w_ref, rest_ref, g_ref, s_ref, sems) = refs[: 2 * side], refs[2 * side :]
    n = g_ref.shape[0]
    steps = n // BLOCK
    slots = g_ref.shape[1] // BLOCK
    share = n // side**2
    part = share // 2
    half = l_ref.shape[1]
    grow, gcol = info_ref[0], info_ref[1]
    copies = []
    for way in range(2):
        for u in range(side):
            for t in range(side):
                di, dj = (shifts[u], shifts[t]) if way == 0 else (shifts[t], shifts[u])
                spot = lax.rem(grow + side - di, side) * side + lax.rem(gcol + side - dj, side)
                to = pl.multiple_of(spot * share + way * part, part)
                copies.append(
                    pltpu.make_async_copy(
                        pieces[way * side + u].at[t * part : (t + 1) * part],
                        g_ref.at[pl.ds(to, part)],
                        sems.at[len(copies)],
                    )
                )
    for copy in copies:
        copy.start()
    for copy in copies:
        copy.wait()

    def place(j):
        return (s_ref, j, j) if j < half else (rest_ref, j - half, j - half)

    for k in range(steps):
        ref, r, c = place(k * BLOCK)
        own = slice(k * BLOCK, (k + 1) * BLOCK)
        for i in range(k, steps):
            if i - k < slots:
                value = g_ref[i * BLOCK : (i + 1) * BLOCK, (i - k) * BLOCK : (i - k + 1) * BLOCK]
            else:
                m = (k - i + steps) * BLOCK
                value = g_ref[own, m : m + BLOCK].T
            ref[r + (i - k) * BLOCK : r + (i - k + 1) * BLOCK, c : c + BLOCK] = value
    sweep(0, half, n, place, l_ref, w_ref)


def second_kernel(rest_ref, l_ref, w_ref, s_ref):
    n = rest_ref.shape[0]
    for k in range(0, n, BLOCK):
        s_ref[k:, k : k + BLOCK] = rest_ref[k:, k : k + BLOCK]
    sweep(0, n, n, lambda j: (s_ref, j, j), l_ref, w_ref)


def shape(*dims):
    return jax.ShapeDtypeStruct(dims, jnp.float32)


def factor_first(info, pieces, n, side, shifts):
    half = n // 2
    slots = n // BLOCK // 2 + 1
    return pl.pallas_call(
        functools.partial(first_kernel, side=side, shifts=shifts),
        name="factor_first",
        out_shape=(shape(n, half), shape(half // BLOCK, BLOCK, BLOCK), shape(half, half)),
        in_specs=[SMEM] + [ANY] * len(pieces),
        out_specs=(VMEM, VMEM, VMEM),
        scratch_shapes=[
            pltpu.VMEM((n, slots * BLOCK), jnp.float32),
            pltpu.VMEM((n, half), jnp.float32),
            pltpu.SemaphoreType.DMA((2 * side**2,)),
        ],
        compiler_params=PARAMS,
        cost_estimate=pl.CostEstimate(
            flops=20 * n**3, bytes_accessed=100 * n * n, transcendentals=0
        ),
    )(info, *pieces)


def factor_second(rest):
    n = rest.shape[0]
    return pl.pallas_call(
        second_kernel,
        name="factor_second",
        out_shape=(shape(n, n), shape(n // BLOCK, BLOCK, BLOCK)),
        in_specs=[VMEM],
        out_specs=(VMEM, VMEM),
        scratch_shapes=[pltpu.VMEM((n, n), jnp.float32)],
        compiler_params=PARAMS,
        cost_estimate=pl.CostEstimate(
            flops=160 * n**3, bytes_accessed=400 * n * n, transcendentals=0
        ),
    )(rest)


def dot_nn(x, y):
    return lax.dot_general(
        x,
        y,
        (((1,), (0,)), ((), ())),
        precision=lax.Precision.HIGHEST,
        preferred_element_type=jnp.float32,
    )


def solve_rows(value_ref, high, low, wide, l0_ref, l1_ref):
    half, n = l1_ref.shape[0], l0_ref.shape[0]
    for j in range(0, n, WIDE):
        e = j + WIDE
        value = value_ref[:, j:e]
        if j:
            c = min(j, half)
            value = value - dot_split((high[:, 0:c], low[:, 0:c]), split(l0_ref[j:e, 0:c]))
        if j > half:
            left = split(l1_ref[j - half : e - half, 0 : j - half])
            value = value - dot_split((high[:, half:j], low[:, half:j]), left)
        value = dot_split(split(value), (wide[0][j // WIDE], wide[1][j // WIDE]))
        value_ref[:, j:e] = value
        high[:, j:e], low[:, j:e] = split(value)


def row_kernel(
    info_ref, l0_ref, l1_ref, w0_ref, w1_ref, row_hbm, p_ref, high, low, wh_ref, wl_ref, o_ref,
    z_ref, rows, zero_sem, row_sem, *, side, blocks
):
    half, n = l1_ref.shape[0], l0_ref.shape[0]
    own = rows.shape[0] // side
    row_from, col_from = 2, 2 + blocks
    load = pltpu.make_async_copy(row_hbm, rows, row_sem)
    load.start()
    z_ref[...] = jnp.zeros_like(z_ref)

    def zeros(act):
        def row(r, _):
            here = pl.ds(pl.multiple_of(r * BLOCK, BLOCK), BLOCK)
            absent = info_ref[row_from + r] < 0

            @pl.when(absent)
            def _():
                act(pltpu.make_async_copy(z_ref, o_ref.at[here], zero_sem))

            @pl.when(jnp.logical_not(absent))
            def _():
                def block(c, _):
                    @pl.when(info_ref[col_from + c] < 0)
                    def _():
                        there = pl.ds(pl.multiple_of(c * BLOCK, BLOCK), BLOCK)
                        act(
                            pltpu.make_async_copy(
                                z_ref.at[:, 0:BLOCK], o_ref.at[here, there], zero_sem
                            )
                        )

                    return 0

                lax.fori_loop(0, blocks, block, 0)

            return 0

        lax.fori_loop(0, blocks, row, 0)

    zeros(lambda copy: copy.start())

    def inverse(k):
        return w0_ref[k] if k < half // BLOCK else w1_ref[k - half // BLOCK]

    zero = jnp.zeros((BLOCK, BLOCK), jnp.float32)
    for j in range(0, n, WIDE):
        mid, e = j + BLOCK, j + WIDE
        w0, w1 = inverse(j // BLOCK), inverse(mid // BLOCK)
        ref, at = (l0_ref, j) if j < half else (l1_ref, j - half)
        base = mid if j < half else mid - half
        cross = dot_nn(w1, dot_nn(ref[base : base + BLOCK, at : at + BLOCK], w0))
        top = jnp.concatenate([w0, zero], axis=1)
        both = jnp.concatenate([top, jnp.concatenate([-cross, w1], axis=1)], axis=0)
        wh_ref[j // WIDE], wl_ref[j // WIDE] = split(both)
    load.wait()
    solve_rows(rows, high, low, (wh_ref, wl_ref), l0_ref, l1_ref)
    p_ref[...] = rows[pl.ds(pl.multiple_of(info_ref[1] * own, own), own), :]
    zeros(lambda copy: copy.wait())


def column_kernel(
    info_ref, l0_ref, l1_ref, rh_ref, rl_ref, wh_ref, wl_ref, *refs, side, shifts, blocks, parts
):
    col_hbm, (t_hbm, _, o_ref, cols, s_ref, high, low, sems) = (
        refs[: parts * side],
        refs[parts * side :],
    )
    m = cols.shape[0]
    own = m // side
    part = own // parts
    count = m // BLOCK
    row_to = 2 + 2 * blocks
    col_to = row_to + count
    loads = []
    for h in range(parts):
        for k in range(side):
            to = lax.rem(info_ref[0] + side - shifts[k], side) * own + h * part
            loads.append(
                pltpu.make_async_copy(
                    col_hbm[h * side + k],
                    cols.at[pl.ds(pl.multiple_of(to, part), part)],
                    sems.at[len(loads)],
                )
            )
    loads.append(pltpu.make_async_copy(t_hbm, s_ref, sems.at[len(loads)]))
    for load in loads:
        load.start()
    for load in loads[:-1]:
        load.wait()
    solve_rows(cols, high, low, (wh_ref, wl_ref), l0_ref, l1_ref)
    loads[-1].wait()
    stores = []
    step = m // 2
    for r in range(0, m, step):
        here = slice(r, r + step)
        s_ref[here, :] = s_ref[here, :] - dot_split(
            (rh_ref[here, :], rl_ref[here, :]), (high[...], low[...])
        )
        for a in range(r // BLOCK, (r + step) // BLOCK):
            there = pl.ds(pl.multiple_of(info_ref[row_to + a] * BLOCK, BLOCK), BLOCK)
            for b in range(count):
                column = pl.ds(pl.multiple_of(info_ref[col_to + b] * BLOCK, BLOCK), BLOCK)
                copy = pltpu.make_async_copy(
                    s_ref.at[a * BLOCK : (a + 1) * BLOCK, b * BLOCK : (b + 1) * BLOCK],
                    o_ref.at[there, column],
                    sems.at[len(loads) + len(stores)],
                )
                copy.start()
                stores.append(copy)
    for copy in stores:
        copy.wait()


def half_shape(*dims):
    return jax.ShapeDtypeStruct(dims, jnp.bfloat16)


def row_part(info, factors, inverses, rows, side, blocks):
    m, n = rows.shape
    return pl.pallas_call(
        functools.partial(row_kernel, side=side, blocks=blocks),
        name="row_part",
        out_shape=(
            shape(m // side, n),
            half_shape(m, n),
            half_shape(m, n),
            half_shape(n // WIDE, WIDE, WIDE),
            half_shape(n // WIDE, WIDE, WIDE),
            shape(blocks * BLOCK, blocks * BLOCK),
        ),
        in_specs=[SMEM] + [VMEM] * 4 + [ANY],
        out_specs=(VMEM,) * 5 + (ANY,),
        scratch_shapes=[
            pltpu.VMEM((BLOCK, blocks * BLOCK), jnp.float32),
            pltpu.VMEM((m, n), jnp.float32),
            pltpu.SemaphoreType.DMA,
            pltpu.SemaphoreType.DMA,
        ],
        compiler_params=PARAMS,
        cost_estimate=pl.CostEstimate(
            flops=6 * m * n * n, bytes_accessed=100 * n * n, transcendentals=0
        ),
    )(info, *factors, *inverses, rows)


def column_part(info, factors, high, low, wide, columns, trailing, spread, side, shifts, blocks):
    m, n = high.shape
    count = m // BLOCK
    inputs = (info, *factors, high, low, *wide, *columns, trailing, spread)
    return pl.pallas_call(
        functools.partial(
            column_kernel, side=side, shifts=shifts, blocks=blocks, parts=len(columns) // side
        ),
        name="column_part",
        out_shape=shape(*spread.shape),
        in_specs=[SMEM] + [VMEM] * 6 + [ANY] * (2 + len(columns)),
        out_specs=ANY,
        input_output_aliases={len(inputs) - 1: 0},
        scratch_shapes=[
            pltpu.VMEM((m, n), jnp.float32),
            pltpu.VMEM((m, m), jnp.float32),
            pltpu.VMEM((m, n), jnp.bfloat16),
            pltpu.VMEM((m, n), jnp.bfloat16),
            pltpu.SemaphoreType.DMA((1 + len(columns) + count**2,)),
        ],
        compiler_params=PARAMS,
        cost_estimate=pl.CostEstimate(
            flops=6 * m * n * (n + m), bytes_accessed=4 * (3 * m * n + n * n), transcendentals=0
        ),
    )(*inputs)


def packed_rows(rows, index, parts):
    n = rows.shape[1]
    steps = n // BLOCK
    slots = steps // 2 + 1
    own = index * steps // parts
    twice = jnp.concatenate([rows, rows], axis=1)
    start = (own + steps - slots + 1) % steps
    turned = lax.dynamic_slice_in_dim(twice, start * BLOCK, slots * BLOCK, 1)
    pieces = [turned[:, (slots - 1 - m) * BLOCK : (slots - m) * BLOCK] for m in range(slots)]
    return jnp.concatenate(pieces, axis=1)


def around(x, axis, shifts):
    size = lax.axis_size(axis)
    return [
        lax.ppermute(x, axis, [(s, (s + t) % size) for s in range(size)]) if t else x
        for t in shifts
    ]


def local(diag_block, lower_block, trailing_block, parent_front, row_map):
    grow, gcol = lax.axis_index("grow"), lax.axis_index("gcol")
    side = lax.axis_size("gcol")
    spot = grow * side + gcol
    shifts = (0,) + tuple(range(2, side - 1)) + (1, side - 1)
    lower = lower_block[0]
    trailing = trailing_block[0]
    n = diag_block.shape[2]
    half = n // 2

    count = trailing.shape[0] // BLOCK
    blocks = parent_front.shape[1] * lax.axis_size("wide") // BLOCK
    mine = lax.dynamic_slice_in_dim(row_map, lax.axis_index("wide"), 1, 0)[0]
    targets = [
        lax.dynamic_slice_in_dim(mine, k * count, count) % blocks for k in (grow, gcol)
    ]
    slots = jnp.arange(blocks, dtype=jnp.int32)[:, None]
    sources = [
        jnp.max(
            jnp.where(to[None, :] == slots, jnp.arange(count, dtype=jnp.int32)[None], -1), axis=1
        )
        for to in targets
    ]
    info = jnp.concatenate([jnp.stack([grow, gcol]).astype(jnp.int32), *sources, *targets])

    swap = [(i * side + j, j * side + i) for i in range(side) for j in range(side)]
    packed = packed_rows(diag_block[0], spot, side * side)
    part = packed.shape[0] // 2
    top = jnp.concatenate(around(packed[:part], "gcol", shifts), axis=0)
    bottom = jnp.concatenate(around(packed[part:], "grow", shifts), axis=0)
    pieces = around(top, "grow", shifts) + around(bottom, "gcol", shifts)
    pieces, lower = lax.optimization_barrier((pieces, lower))
    cut = lower.shape[0] // 2
    early = lax.ppermute(lower[:cut], ("grow", "gcol"), swap)
    late = lax.ppermute(lower[cut:], ("grow", "gcol"), swap)
    rows = lax.all_gather(lower, "gcol", axis=0, tiled=True)
    l0, w0, rest = factor_first(info, pieces, n, side, shifts)
    rest, early = lax.optimization_barrier((rest, early))
    columns = around(early, "grow", shifts)
    l1, w1 = factor_second(rest)
    l1, late = lax.optimization_barrier((l1, late))
    rows, columns = lax.optimization_barrier((rows, columns))
    columns = columns + around(late, "grow", shifts)
    share = diag_block.shape[1]
    own_rows = lax.dynamic_slice_in_dim(l0, spot * share, share, 0)
    from_half = jnp.maximum(spot * share - half, 0)
    right = lax.dynamic_slice_in_dim(l1, from_half, share, 0)
    right = jnp.where(spot * share >= half, right, 0.0)
    factor_rows = jnp.concatenate([own_rows, right], axis=1)

    panel, high, low, wide_high, wide_low, spread = row_part(
        info, (l0, l1), (w0, w1), rows, side, blocks
    )
    spread = column_part(
        info, (l0, l1), high, low, (wide_high, wide_low), columns, trailing, spread,
        side, shifts, blocks,
    )
    summed = lax.psum_scatter(spread, "wide", scatter_dimension=0, tiled=True)
    parent = parent_front + summed[None]
    return factor_rows[None], panel[None], parent


def solution(mesh):
    placed = (
        P("wide", ("grow", "gcol"), None),
        P("wide", ("grow", "gcol"), None),
        P("wide", "grow", "gcol"),
        P("grow", "wide", "gcol"),
        P(),
    )
    return jax.shard_map(
        local,
        mesh=mesh,
        in_specs=placed,
        out_specs=(
            P("wide", ("grow", "gcol"), None),
            P("wide", ("grow", "gcol"), None),
            P("grow", "wide", "gcol"),
        ),
        check_vma=False,
    )
```

```python
import functools

import jax
import jax.numpy as jnp
from jax import lax
from jax.experimental import pallas as pl
from jax.experimental.pallas import tpu as pltpu
from jax.sharding import PartitionSpec as P

BLOCK = 128
WIDE = 256
SUB = 8
VMEM = pl.BlockSpec(memory_space=pltpu.VMEM)
ANY = pl.BlockSpec(memory_space=pl.ANY)
SMEM = pl.BlockSpec(memory_space=pltpu.SMEM)
PARAMS = pltpu.CompilerParams(vmem_limit_bytes=56 * 2**20)


def dot_nt(x, y):
    return lax.dot_general(
        x,
        y,
        (((1,), (1,)), ((), ())),
        precision=lax.Precision.HIGHEST,
        preferred_element_type=jnp.float32,
    )


def split(x):
    high = x.astype(jnp.bfloat16)
    return high, (x - high.astype(jnp.float32)).astype(jnp.bfloat16)


def dot_split(x, y):
    def one(a, b):
        return lax.dot_general(
            a, b, (((1,), (1,)), ((), ())), preferred_element_type=jnp.float32
        )

    return one(x[0], y[0]) + (one(x[0], y[1]) + one(x[1], y[0]))


def factor_block(rows):
    count = len(rows)
    shape = (SUB, BLOCK)
    lane = lax.broadcasted_iota(jnp.int32, shape, 1)
    sub = lax.broadcasted_iota(jnp.int32, shape, 0)
    left = list(rows)
    right = [jnp.where(lane == sub + SUB * b, 1.0, 0.0).astype(jnp.float32) for b in range(count)]

    def along_lanes(x, j):
        return jnp.broadcast_to(x[:, j : j + 1], shape)

    def along_rows(x, j):
        return jnp.broadcast_to(x[j : j + 1, :], shape)

    for b in range(count):
        columns = [along_lanes(left[b], SUB * b + j) for j in range(SUB)]
        t = [[along_rows(columns[j], i) for j in range(i + 1)] for i in range(SUB)]
        inverse = []
        for j in range(SUB):
            inverse.append(lax.rsqrt(t[j][j]))
            for i in range(j + 1, SUB):
                t[i][j] = t[i][j] * inverse[j]
            for i in range(j + 1, SUB):
                for k in range(j + 1, i + 1):
                    t[i][k] = t[i][k] - t[i][j] * t[k][j]

        def solve(values):
            out = []
            for j in range(SUB):
                value = values[j]
                for k in range(j):
                    value = value - t[j][k] * out[k]
                out.append(value * inverse[j])
            return out

        upper = solve([along_rows(left[b], j) for j in range(SUB)])
        lower = solve([along_rows(right[b], j) for j in range(SUB)])
        left_b, right_b = upper[0], lower[0]
        for j in range(1, SUB):
            left_b = jnp.where(sub == j, upper[j], left_b)
            right_b = jnp.where(sub == j, lower[j], right_b)
        left[b], right[b] = left_b, right_b
        for c in range(b + 1, count):
            scale = solve([along_lanes(left[c], SUB * b + j) for j in range(SUB)])
            for j in range(SUB):
                left[c] = left[c] - scale[j] * upper[j]
                right[c] = right[c] - scale[j] * lower[j]
    return left, right


def sweep(start, stop, end, place, l_ref, w_ref):
    ii = lax.broadcasted_iota(jnp.int32, (BLOCK, BLOCK), 0)
    jj = lax.broadcasted_iota(jnp.int32, (BLOCK, BLOCK), 1)
    for o in range(start, stop, BLOCK):
        e = o + BLOCK
        ref, r, c = place(o)
        upper, inverse = factor_block(
            [ref[r + k : r + k + SUB, c : c + BLOCK] for k in range(0, BLOCK, SUB)]
        )
        at = slice(o - start, e - start)
        l_ref[at, at] = jnp.where(ii >= jj, jnp.concatenate(upper, axis=0).T, 0.0)
        inverse = jnp.concatenate(inverse, axis=0)
        w_ref[(o - start) // BLOCK] = inverse
        if o > start:
            l_ref[0 : o - start, at] = jnp.zeros((o - start, BLOCK), jnp.float32)
        if e == end:
            break
        below = dot_nt(ref[r + BLOCK : r + end - o, c : c + BLOCK], inverse)
        l_ref[e - start :, at] = below
        for j in range(e, end, BLOCK):
            update = dot_nt(below[j - e :], below[j - e : j - e + BLOCK])
            ref, r, c = place(j)
            here = (slice(r, r + end - j), slice(c, c + BLOCK))
            ref[here] = ref[here] - update


def first_kernel(info_ref, *refs, side, shifts):
    pieces, (l_ref, w_ref, rest_ref, g_ref, s_ref, sems) = refs[: 2 * side], refs[2 * side :]
    n = g_ref.shape[0]
    steps = n // BLOCK
    slots = g_ref.shape[1] // BLOCK
    share = n // side**2
    part = share // 2
    half = l_ref.shape[1]
    grow, gcol = info_ref[0], info_ref[1]
    copies = []
    for way in range(2):
        for u in range(side):
            for t in range(side):
                di, dj = (shifts[u], shifts[t]) if way == 0 else (shifts[t], shifts[u])
                spot = lax.rem(grow + side - di, side) * side + lax.rem(gcol + side - dj, side)
                to = pl.multiple_of(spot * share + way * part, part)
                copies.append(
                    pltpu.make_async_copy(
                        pieces[way * side + u].at[t * part : (t + 1) * part],
                        g_ref.at[pl.ds(to, part)],
                        sems.at[len(copies)],
                    )
                )
    for copy in copies:
        copy.start()
    for copy in copies:
        copy.wait()

    def place(j):
        return (s_ref, j, j) if j < half else (rest_ref, j - half, j - half)

    for k in range(steps):
        ref, r, c = place(k * BLOCK)
        own = slice(k * BLOCK, (k + 1) * BLOCK)
        for i in range(k, steps):
            if i - k < slots:
                value = g_ref[i * BLOCK : (i + 1) * BLOCK, (i - k) * BLOCK : (i - k + 1) * BLOCK]
            else:
                m = (k - i + steps) * BLOCK
                value = g_ref[own, m : m + BLOCK].T
            ref[r + (i - k) * BLOCK : r + (i - k + 1) * BLOCK, c : c + BLOCK] = value
    sweep(0, half, n, place, l_ref, w_ref)


def second_kernel(info_ref, rest_ref, l_ref, w_ref, o_ref, s_ref, z_ref, zero_sem, *, blocks):
    n = rest_ref.shape[0]
    row_from, col_from = 2, 2 + blocks
    z_ref[...] = jnp.zeros_like(z_ref)

    def zeros(act):
        def row(r, _):
            here = pl.ds(pl.multiple_of(r * BLOCK, BLOCK), BLOCK)
            absent = info_ref[row_from + r] < 0

            @pl.when(absent)
            def _():
                act(pltpu.make_async_copy(z_ref, o_ref.at[here], zero_sem))

            @pl.when(jnp.logical_not(absent))
            def _():
                def block(c, _):
                    @pl.when(info_ref[col_from + c] < 0)
                    def _():
                        there = pl.ds(pl.multiple_of(c * BLOCK, BLOCK), BLOCK)
                        act(
                            pltpu.make_async_copy(
                                z_ref.at[:, 0:BLOCK], o_ref.at[here, there], zero_sem
                            )
                        )

                    return 0

                lax.fori_loop(0, blocks, block, 0)

            return 0

        lax.fori_loop(0, blocks, row, 0)

    zeros(lambda copy: copy.start())
    for k in range(0, n, BLOCK):
        s_ref[k:, k : k + BLOCK] = rest_ref[k:, k : k + BLOCK]
    sweep(0, n, n, lambda j: (s_ref, j, j), l_ref, w_ref)
    zeros(lambda copy: copy.wait())


def shape(*dims):
    return jax.ShapeDtypeStruct(dims, jnp.float32)


def factor_first(info, pieces, n, side, shifts):
    half = n // 2
    slots = n // BLOCK // 2 + 1
    return pl.pallas_call(
        functools.partial(first_kernel, side=side, shifts=shifts),
        name="factor_first",
        out_shape=(shape(n, half), shape(half // BLOCK, BLOCK, BLOCK), shape(half, half)),
        in_specs=[SMEM] + [ANY] * len(pieces),
        out_specs=(VMEM, VMEM, VMEM),
        scratch_shapes=[
            pltpu.VMEM((n, slots * BLOCK), jnp.float32),
            pltpu.VMEM((n, half), jnp.float32),
            pltpu.SemaphoreType.DMA((2 * side**2,)),
        ],
        compiler_params=PARAMS,
        cost_estimate=pl.CostEstimate(
            flops=20 * n**3, bytes_accessed=100 * n * n, transcendentals=0
        ),
    )(info, *pieces)


def factor_second(info, rest, blocks):
    n = rest.shape[0]
    return pl.pallas_call(
        functools.partial(second_kernel, blocks=blocks),
        name="factor_second",
        out_shape=(
            shape(n, n),
            shape(n // BLOCK, BLOCK, BLOCK),
            shape(blocks * BLOCK, blocks * BLOCK),
        ),
        in_specs=[SMEM, VMEM],
        out_specs=(VMEM, VMEM, ANY),
        scratch_shapes=[
            pltpu.VMEM((n, n), jnp.float32),
            pltpu.VMEM((BLOCK, blocks * BLOCK), jnp.float32),
            pltpu.SemaphoreType.DMA,
        ],
        compiler_params=PARAMS,
        cost_estimate=pl.CostEstimate(
            flops=160 * n**3, bytes_accessed=400 * n * n, transcendentals=0
        ),
    )(info, rest)


def dot_nn(x, y):
    return lax.dot_general(
        x,
        y,
        (((1,), (0,)), ((), ())),
        precision=lax.Precision.HIGHEST,
        preferred_element_type=jnp.float32,
    )


def solve_rows(value_ref, high, low, wide, l0_ref, l1_ref):
    half, n = l1_ref.shape[0], l0_ref.shape[0]
    for j in range(0, n, WIDE):
        e = j + WIDE
        value = value_ref[:, j:e]
        if j:
            c = min(j, half)
            value = value - dot_split((high[:, 0:c], low[:, 0:c]), split(l0_ref[j:e, 0:c]))
        if j > half:
            left = split(l1_ref[j - half : e - half, 0 : j - half])
            value = value - dot_split((high[:, half:j], low[:, half:j]), left)
        value = dot_split(split(value), (wide[0][j // WIDE], wide[1][j // WIDE]))
        value_ref[:, j:e] = value
        high[:, j:e], low[:, j:e] = split(value)


def row_kernel(
    info_ref, l0_ref, l1_ref, w0_ref, w1_ref, row_hbm, p_ref, f_ref, high, low, wh_ref, wl_ref,
    rows, row_sem, *, side
):
    half, n = l1_ref.shape[0], l0_ref.shape[0]
    own = rows.shape[0] // side
    load = pltpu.make_async_copy(row_hbm, rows, row_sem)
    load.start()

    def inverse(k):
        return w0_ref[k] if k < half // BLOCK else w1_ref[k - half // BLOCK]

    zero = jnp.zeros((BLOCK, BLOCK), jnp.float32)
    for j in range(0, n, WIDE):
        mid, e = j + BLOCK, j + WIDE
        w0, w1 = inverse(j // BLOCK), inverse(mid // BLOCK)
        ref, at = (l0_ref, j) if j < half else (l1_ref, j - half)
        base = mid if j < half else mid - half
        cross = dot_nn(w1, dot_nn(ref[base : base + BLOCK, at : at + BLOCK], w0))
        top = jnp.concatenate([w0, zero], axis=1)
        both = jnp.concatenate([top, jnp.concatenate([-cross, w1], axis=1)], axis=0)
        wh_ref[j // WIDE], wl_ref[j // WIDE] = split(both)
    share = f_ref.shape[0]
    first = (info_ref[0] * side + info_ref[1]) * share
    f_ref[:, 0:half] = l0_ref[pl.ds(pl.multiple_of(first, share), share), :]
    second = pl.multiple_of(jnp.maximum(first - half, 0), share)
    f_ref[:, half:n] = jnp.where(first >= half, l1_ref[pl.ds(second, share), :], 0.0)
    load.wait()
    solve_rows(rows, high, low, (wh_ref, wl_ref), l0_ref, l1_ref)
    p_ref[...] = rows[pl.ds(pl.multiple_of(info_ref[1] * own, own), own), :]


def column_kernel(
    info_ref, l0_ref, l1_ref, rh_ref, rl_ref, wh_ref, wl_ref, *refs, side, shifts, blocks, parts
):
    col_hbm, (t_hbm, _, o_ref, cols, s_ref, high, low, sems) = (
        refs[: parts * side],
        refs[parts * side :],
    )
    m = cols.shape[0]
    own = m // side
    part = own // parts
    count = m // BLOCK
    row_to = 2 + 2 * blocks
    col_to = row_to + count
    loads = []
    for h in range(parts):
        for k in range(side):
            to = lax.rem(info_ref[0] + side - shifts[k], side) * own + h * part
            loads.append(
                pltpu.make_async_copy(
                    col_hbm[h * side + k],
                    cols.at[pl.ds(pl.multiple_of(to, part), part)],
                    sems.at[len(loads)],
                )
            )
    loads.append(pltpu.make_async_copy(t_hbm, s_ref, sems.at[len(loads)]))
    for load in loads:
        load.start()
    for load in loads[:-1]:
        load.wait()
    solve_rows(cols, high, low, (wh_ref, wl_ref), l0_ref, l1_ref)
    loads[-1].wait()
    stores = []
    step = m // 2
    for r in range(0, m, step):
        here = slice(r, r + step)
        s_ref[here, :] = s_ref[here, :] - dot_split(
            (rh_ref[here, :], rl_ref[here, :]), (high[...], low[...])
        )
        for a in range(r // BLOCK, (r + step) // BLOCK):
            there = pl.ds(pl.multiple_of(info_ref[row_to + a] * BLOCK, BLOCK), BLOCK)
            for b in range(count):
                column = pl.ds(pl.multiple_of(info_ref[col_to + b] * BLOCK, BLOCK), BLOCK)
                copy = pltpu.make_async_copy(
                    s_ref.at[a * BLOCK : (a + 1) * BLOCK, b * BLOCK : (b + 1) * BLOCK],
                    o_ref.at[there, column],
                    sems.at[len(loads) + len(stores)],
                )
                copy.start()
                stores.append(copy)
    for copy in stores:
        copy.wait()


def half_shape(*dims):
    return jax.ShapeDtypeStruct(dims, jnp.bfloat16)


def row_part(info, factors, inverses, rows, side):
    m, n = rows.shape
    return pl.pallas_call(
        functools.partial(row_kernel, side=side),
        name="row_part",
        out_shape=(
            shape(m // side, n),
            shape(n // side**2, n),
            half_shape(m, n),
            half_shape(m, n),
            half_shape(n // WIDE, WIDE, WIDE),
            half_shape(n // WIDE, WIDE, WIDE),
        ),
        in_specs=[SMEM] + [VMEM] * 4 + [ANY],
        out_specs=(VMEM,) * 6,
        scratch_shapes=[
            pltpu.VMEM((m, n), jnp.float32),
            pltpu.SemaphoreType.DMA,
        ],
        compiler_params=PARAMS,
        cost_estimate=pl.CostEstimate(
            flops=6 * m * n * n, bytes_accessed=100 * n * n, transcendentals=0
        ),
    )(info, *factors, *inverses, rows)


def column_part(info, factors, high, low, wide, columns, trailing, spread, side, shifts, blocks):
    m, n = high.shape
    count = m // BLOCK
    inputs = (info, *factors, high, low, *wide, *columns, trailing, spread)
    return pl.pallas_call(
        functools.partial(
            column_kernel, side=side, shifts=shifts, blocks=blocks, parts=len(columns) // side
        ),
        name="column_part",
        out_shape=shape(*spread.shape),
        in_specs=[SMEM] + [VMEM] * 6 + [ANY] * (2 + len(columns)),
        out_specs=ANY,
        input_output_aliases={len(inputs) - 1: 0},
        scratch_shapes=[
            pltpu.VMEM((m, n), jnp.float32),
            pltpu.VMEM((m, m), jnp.float32),
            pltpu.VMEM((m, n), jnp.bfloat16),
            pltpu.VMEM((m, n), jnp.bfloat16),
            pltpu.SemaphoreType.DMA((1 + len(columns) + count**2,)),
        ],
        compiler_params=PARAMS,
        cost_estimate=pl.CostEstimate(
            flops=6 * m * n * (n + m), bytes_accessed=4 * (3 * m * n + n * n), transcendentals=0
        ),
    )(*inputs)


def packed_rows(rows, index, parts):
    n = rows.shape[1]
    steps = n // BLOCK
    slots = steps // 2 + 1
    own = index * steps // parts
    twice = jnp.concatenate([rows, rows], axis=1)
    start = (own + steps - slots + 1) % steps
    turned = lax.dynamic_slice_in_dim(twice, start * BLOCK, slots * BLOCK, 1)
    pieces = [turned[:, (slots - 1 - m) * BLOCK : (slots - m) * BLOCK] for m in range(slots)]
    return jnp.concatenate(pieces, axis=1)


def around(x, axis, shifts):
    size = lax.axis_size(axis)
    return [
        lax.ppermute(x, axis, [(s, (s + t) % size) for s in range(size)]) if t else x
        for t in shifts
    ]


def local(diag_block, lower_block, trailing_block, parent_front, row_map):
    grow, gcol = lax.axis_index("grow"), lax.axis_index("gcol")
    side = lax.axis_size("gcol")
    spot = grow * side + gcol
    shifts = (0,) + tuple(range(2, side - 1)) + (1, side - 1)
    lower = lower_block[0]
    trailing = trailing_block[0]
    n = diag_block.shape[2]

    count = trailing.shape[0] // BLOCK
    blocks = parent_front.shape[1] * lax.axis_size("wide") // BLOCK
    mine = lax.dynamic_slice_in_dim(row_map, lax.axis_index("wide"), 1, 0)[0]
    targets = [
        lax.dynamic_slice_in_dim(mine, k * count, count) % blocks for k in (grow, gcol)
    ]
    slots = jnp.arange(blocks, dtype=jnp.int32)[:, None]
    sources = [
        jnp.max(
            jnp.where(to[None, :] == slots, jnp.arange(count, dtype=jnp.int32)[None], -1), axis=1
        )
        for to in targets
    ]
    info = jnp.concatenate([jnp.stack([grow, gcol]).astype(jnp.int32), *sources, *targets])

    swap = [(i * side + j, j * side + i) for i in range(side) for j in range(side)]
    packed = packed_rows(diag_block[0], spot, side * side)
    part = packed.shape[0] // 2
    top, bottom, info = lax.optimization_barrier(
        (around(packed[:part], "gcol", shifts), around(packed[part:], "grow", shifts), info)
    )
    top, bottom = jnp.concatenate(top, axis=0), jnp.concatenate(bottom, axis=0)
    pieces = around(top, "grow", shifts) + around(bottom, "gcol", shifts)
    pieces, lower = lax.optimization_barrier((pieces, lower))
    cut = lower.shape[0] // 2
    early = lax.ppermute(lower[:cut], ("grow", "gcol"), swap)
    late = lax.ppermute(lower[cut:], ("grow", "gcol"), swap)
    rows = lax.all_gather(lower, "gcol", axis=0, tiled=True)
    l0, w0, rest = factor_first(info, pieces, n, side, shifts)
    rest, early = lax.optimization_barrier((rest, early))
    columns = around(early, "grow", shifts)
    l1, w1, spread = factor_second(info, rest, blocks)
    l1, late = lax.optimization_barrier((l1, late))
    rows, columns = lax.optimization_barrier((rows, columns))
    columns = columns + around(late, "grow", shifts)
    panel, factor_rows, high, low, wide_high, wide_low = row_part(
        info, (l0, l1), (w0, w1), rows, side
    )
    spread = column_part(
        info, (l0, l1), high, low, (wide_high, wide_low), columns, trailing, spread,
        side, shifts, blocks,
    )
    summed = lax.psum_scatter(spread, "wide", scatter_dimension=0, tiled=True)
    parent = parent_front + summed[None]
    return factor_rows[None], panel[None], parent


def solution(mesh):
    placed = (
        P("wide", ("grow", "gcol"), None),
        P("wide", ("grow", "gcol"), None),
        P("wide", "grow", "gcol"),
        P("grow", "wide", "gcol"),
        P(),
    )
    return jax.shard_map(
        local,
        mesh=mesh,
        in_specs=placed,
        out_specs=(
            P("wide", ("grow", "gcol"), None),
            P("wide", ("grow", "gcol"), None),
            P("grow", "wide", "gcol"),
        ),
        check_vma=False,
    )
```
